512 devices in a mesh: sec: 32 (over z, core), bond: 16 (over y, x).
Axes of the slice: x: 4, y: 4, z: 16, core: 2. Of those that a mesh axis runs over, the one named last changes fastest.
Arguments:
- left_env: bfloat16 [32, 512, 8, 512], P('sec', 'bond'), may hold values from -6 to 6
- site: bfloat16 [32, 512, 4, 512], P('sec', 'bond'), may hold values from -0.125 to 0.125
- psi: bfloat16 [32, 512, 4, 4, 512], P('sec', 'bond'), may hold values from -0.25 to 0.25
- right_env: bfloat16 [32, 8, 512, 512], P('sec'), may hold values from -0.09375 to 0.09375
- mpo: bfloat16 [8, 8, 4, 4], replicated, may hold values from -1 to 1
Outputs:
- new_left: bfloat16 [32, 512, 8, 512], P('sec', 'bond')
- product: bfloat16 [32, 512, 4, 4, 512], P('sec', 'bond')
The draws below stay inside these ranges and needn't reach their ends.
All inputs are finite; a program needn't handle non-finite values.
Results may differ from the reference program's by a relative error of at most 0.0095.
Values may be sent and summed in bfloat16 or wider, within the bound.
No kernel may reach another device: no remote copies, remote signals or barrier semaphores. Data moves between devices by JAX's collectives and lax.ppermute only.
A program may use at most 64 MiB of HBM per device.

```python
import jax
import jax.numpy as jnp
from jax import lax

CHI = 512
MPO_W = 8
PHYS = 4
SECTIONS = 32


def level_of(stream_key, extent, cuts, low, high):
    factor_of = 1.0
    for dim, parts in cuts:
        heights = jax.random.uniform(jax.random.fold_in(jax.random.fold_in(stream_key, 6), dim), (parts,), jnp.float32, low / len(cuts), high / len(cuts))
        factor_of = factor_of * jnp.repeat(jnp.exp(heights), extent[dim] // parts).reshape((-1,) + (1,) * (len(extent) - 1 - dim))
    return factor_of


def gaussian(key, shape, spread, reach, pieces=(), held_as=jnp.bfloat16):
    drawn = jax.random.normal(key, shape, jnp.float32) * spread
    if len(pieces) > 0:
        drawn = level_of(key, shape, pieces, -0.22, 0.18) * drawn
    return jnp.clip(drawn, min=-reach, max=reach).astype(held_as)


def setup_inputs(seed: int = 0) -> dict:
    arg_keys = jax.random.split(jax.random.key(seed), 6)
    return {
        "left_env": gaussian(arg_keys[0], (SECTIONS, CHI, MPO_W, CHI), 1.0, 6.0, ((0, 32), (1, 16))),
        "site": gaussian(arg_keys[1], (SECTIONS, CHI, PHYS, CHI), (CHI * PHYS) ** -0.5, 0.125, ((0, 32), (1, 16))),
        "psi": gaussian(arg_keys[2], (SECTIONS, CHI, PHYS, PHYS, CHI), CHI ** -0.5, 0.25, ((0, 32), (1, 16))),
        "right_env": gaussian(arg_keys[3], (SECTIONS, MPO_W, CHI, CHI), (MPO_W * CHI) ** -0.5, 0.09375, ((0, 32),)),
        "mpo": gaussian(arg_keys[4], (MPO_W, MPO_W, PHYS, PHYS), (MPO_W * PHYS) ** -0.5, 1.0),
    }


def reference(left_env, site, psi, right_env, mpo):
    mpo_wide = mpo.astype(jnp.float32)

    def update(pair):
        left, tensor = pair
        first = jnp.dot(left.reshape(CHI * MPO_W, CHI), tensor.reshape(CHI, PHYS * CHI), preferred_element_type=jnp.float32)
        first = first.astype(jnp.bfloat16).reshape(CHI, MPO_W, PHYS, CHI)
        second = jnp.einsum("pmsb,mnsu->punb", first.astype(jnp.float32), mpo_wide).astype(jnp.bfloat16)
        fresh = jnp.dot(tensor.reshape(CHI * PHYS, CHI).T, second.reshape(CHI * PHYS, MPO_W * CHI), preferred_element_type=jnp.float32)
        return fresh.astype(jnp.bfloat16).reshape(CHI, MPO_W, CHI)

    new_left = lax.map(update, (left_env, site))
    two_site = jnp.einsum("mnsu,nkvw->msvuwk", mpo_wide, mpo_wide).astype(jnp.bfloat16).reshape(MPO_W * PHYS * PHYS, PHYS * PHYS * MPO_W)

    def apply(triple):
        left, pair, right = triple
        mixed = jnp.dot(left.reshape(CHI * MPO_W, CHI), pair.reshape(CHI, PHYS * PHYS * CHI), preferred_element_type=jnp.float32)
        mixed = mixed.astype(jnp.bfloat16).reshape(CHI, MPO_W * PHYS * PHYS, CHI)
        projected = jnp.einsum("pqc,qr->prc", mixed.astype(jnp.float32), two_site.astype(jnp.float32)).astype(jnp.bfloat16)
        result = jnp.dot(projected.reshape(CHI * PHYS * PHYS, MPO_W * CHI), right.reshape(MPO_W * CHI, CHI), preferred_element_type=jnp.float32)
        return result.astype(jnp.bfloat16).reshape(CHI, PHYS, PHYS, CHI)

    product = lax.map(apply, (jnp.roll(new_left, 1, axis=0), jnp.roll(psi, 1, axis=0), right_env))
    return new_left, product
```

```python
import jax
import jax.numpy as jnp
from jax import lax
from jax.experimental import pallas as pl
from jax.experimental.pallas import tpu as pltpu
from jax.sharding import PartitionSpec as P

BF = jnp.bfloat16
F32 = jnp.float32
VM = pl.BlockSpec(memory_space=pltpu.VMEM)


def shifted(block, axis, distance):
    devices = range(lax.axis_size(axis))
    route = [((i - distance) % len(devices), i) for i in devices]
    return lax.ppermute(block, axis, route)


def front(left_a, left_b, cols, kron, site_a, site_b, out, first, second):
    for g, left in enumerate((left_a, left_b)):
        rows = left[...]
        for h in range(2):
            part = []
            for s in (2 * h, 2 * h + 1):
                f = jnp.dot(rows, cols[:, s].reshape(512, 256), preferred_element_type=F32)
                part.append(f.reshape(32, 8, 256))
            first[32 * g : 32 * g + 32, 16 * h : 16 * h + 16, :] = jnp.concatenate(part, axis=1).astype(BF)
    for blk in range(8):
        f = first[8 * blk : 8 * blk + 8].reshape(256, 256)
        o = jnp.dot(kron[...], f, preferred_element_type=F32)
        second[:, 32 * blk : 32 * blk + 32, :] = o.astype(BF).reshape(8, 32, 256)
    site = jnp.concatenate([site_a[...], site_b[...]], axis=0)
    for n in range(8):
        o = lax.dot_general(site, second[n], (((0,), (0,)), ((), ())), preferred_element_type=F32)
        out[:, n] = o.astype(BF).reshape(16, 32, 256)


def back(left, pair, mix, right, out, mixed, proj):
    j = pl.program_id(0)
    m = jnp.dot(left[...], pair[...], preferred_element_type=F32)
    m = jnp.concatenate([m[:, :512].reshape(32, 8, 512), m[:, 512:].reshape(32, 8, 512)], axis=1)
    mixed[:, pl.ds(pl.multiple_of(16 * j, 16), 16), :] = m.astype(BF)

    @pl.when(j == 7)
    def _():
        for p in range(32):
            o = jnp.dot(mix[...], mixed[p], preferred_element_type=F32).astype(BF)
            proj[:, 16 * p : 16 * p + 16, :] = o.reshape(8, 16, 512)
        acc = jnp.dot(proj[0], right[0], preferred_element_type=F32)
        for k in range(1, 8):
            acc += jnp.dot(proj[k], right[k], preferred_element_type=F32)
        out[...] = acc.astype(BF)


def shards(left_env, site, psi, right_env, mpo):
    chi = site.shape[-1]
    pair = shifted(psi[0].reshape(32, 16 * chi), "sec", 1)
    pair = lax.all_gather(pair, "bond", axis=0, tiled=True)
    left = left_env[0].reshape(256, chi)
    tensor = site[0].reshape(128, chi)
    swap = [(i, i ^ 1) for i in range(16)]
    left_b = lax.ppermute(left, "bond", swap)
    tensor_b = lax.ppermute(tensor, "bond", swap)
    halves = site[0].reshape(32, 4, 2, 256).transpose(2, 1, 0, 3)
    send = jnp.broadcast_to(halves[None], (8, 2, 4, 32, 256)).reshape(16, 4, 32, 256)
    cols = lax.all_to_all(send, "bond", 0, 0, tiled=True)
    eye = jnp.eye(8, dtype=BF)
    kron = jnp.einsum("pq,mnsu->npuqsm", eye, mpo).reshape(256, 256)
    fresh = pl.pallas_call(
        front,
        out_shape=jax.ShapeDtypeStruct((16, 8, 32, 256), BF),
        in_specs=[VM] * 6,
        out_specs=VM,
        scratch_shapes=[pltpu.VMEM((64, 32, 256), BF), pltpu.VMEM((8, 256, 256), BF)],
        compiler_params=pltpu.CompilerParams(vmem_limit_bytes=40 << 20),
        cost_estimate=pl.CostEstimate(flops=2_000_000_000, bytes_accessed=5_000_000, transcendentals=0),
        name="front",
    )(left, left_b, cols, kron, tensor, tensor_b)
    fresh = lax.all_to_all(fresh, "bond", 0, 0, tiled=True)
    fresh = jnp.sum(fresh.reshape(8, 2, 8, 32, 256).astype(F32), axis=0).astype(BF)
    new_left = fresh.transpose(2, 1, 0, 3).reshape(32, 8, chi)
    source = shifted(new_left.reshape(256, chi), "sec", 1)
    two_site = jnp.einsum("mnsu,nkvw->kuwsvm", mpo, mpo, preferred_element_type=F32)
    two_site = two_site.astype(BF).reshape(128, 128)
    result = pl.pallas_call(
        back,
        grid=(8,),
        out_shape=jax.ShapeDtypeStruct((512, chi), BF),
        in_specs=[
            pl.BlockSpec((256, 512), lambda j: (0, 0)),
            pl.BlockSpec((512, 1024), lambda j: (0, j)),
            pl.BlockSpec((128, 128), lambda j: (0, 0)),
            pl.BlockSpec((8, 512, 512), lambda j: (0, 0, 0)),
        ],
        out_specs=pl.BlockSpec((512, 512), lambda j: (0, 0)),
        scratch_shapes=[pltpu.VMEM((32, 128, 512), BF), pltpu.VMEM((8, 512, 512), BF)],
        compiler_params=pltpu.CompilerParams(vmem_limit_bytes=48 << 20),
        cost_estimate=pl.CostEstimate(flops=5_000_000_000, bytes_accessed=14_000_000, transcendentals=0),
        name="back",
    )(source, pair, two_site, right_env[0])
    return (new_left[None], result.reshape(1, 32, 4, 4, chi))


def solution(mesh):
    in_specs = (
        P("sec", "bond", None, None),
        P("sec", "bond", None, None),
        P("sec", "bond", None, None, None),
        P("sec", None, None, None),
        P(),
    )
    out_specs = (P("sec", "bond", None, None), P("sec", "bond", None, None, None))
    return jax.shard_map(shards, mesh=mesh, in_specs=in_specs, out_specs=out_specs, check_vma=False)
```

```python
import jax
import jax.numpy as jnp
from jax import lax
from jax.experimental import pallas as pl
from jax.experimental.pallas import tpu as pltpu
from jax.sharding import PartitionSpec as P

BF = jnp.bfloat16
F32 = jnp.float32
VM = pl.BlockSpec(memory_space=pltpu.VMEM)


def shifted(block, axis, distance):
    devices = range(lax.axis_size(axis))
    route = [((i - distance) % len(devices), i) for i in devices]
    return lax.ppermute(block, axis, route)


def front(gathered, cols, kron, out, first, second):
    ket = jnp.concatenate([cols[:, s].reshape(512, 128) for s in range(4)], axis=1)
    for g in range(4):
        f = jnp.dot(gathered[g, :256, :], ket, preferred_element_type=F32)
        for h in range(2):
            part = [f[:, 128 * s : 128 * s + 128].reshape(32, 8, 128) for s in (2 * h, 2 * h + 1)]
            first[32 * g : 32 * g + 32, 16 * h : 16 * h + 16, :] = jnp.concatenate(part, axis=1).astype(BF)
    for blk in range(0, 16, 2):
        f = [first[8 * i : 8 * i + 8].reshape(256, 128) for i in (blk, blk + 1)]
        o = jnp.dot(kron[...], jnp.concatenate(f, axis=1), preferred_element_type=F32).astype(BF)
        for i in range(2):
            second[:, 32 * (blk + i) : 32 * (blk + i) + 32, :] = o[:, 128 * i : 128 * i + 128].reshape(8, 32, 128)
    site = gathered[:, 256:, :].reshape(512, 512)
    for n in range(0, 8, 2):
        f = jnp.concatenate([second[n], second[n + 1]], axis=1)
        o = lax.dot_general(site, f, (((0,), (0,)), ((), ())), preferred_element_type=F32).astype(BF)
        for i in range(2):
            out[:, n + i] = o[:, 128 * i : 128 * i + 128].reshape(16, 32, 128)


def back(left, pair, mix, right, out, mixed, proj, env, sem):
    j = pl.program_id(0)
    fetch = pltpu.make_async_copy(right, env, sem)

    @pl.when(j == 0)
    def _():
        fetch.start()

    m = jnp.dot(left[...], pair[...], preferred_element_type=F32)
    m = jnp.concatenate([m[:, :512].reshape(32, 8, 512), m[:, 512:].reshape(32, 8, 512)], axis=1)
    mixed[:, pl.ds(pl.multiple_of(16 * j, 16), 16), :] = m.astype(BF)

    @pl.when(j == 7)
    def _():
        for p in range(32):
            o = jnp.dot(mix[...], mixed[p], preferred_element_type=F32).astype(BF)
            for k in range(8):
                proj[16 * p : 16 * p + 16, 512 * k : 512 * k + 512] = o[16 * k : 16 * k + 16, :]
        fetch.wait()
        out[...] = jnp.dot(proj[...], env[...], preferred_element_type=F32).astype(BF)


def shards(left_env, site, psi, right_env, mpo):
    chi = site.shape[-1]
    pair = shifted(psi[0], "sec", 1).reshape(32, 16 * chi)
    pair = lax.all_gather(pair, "bond", axis=0, tiled=True)
    own = jnp.concatenate([left_env[0].reshape(256, chi), site[0].reshape(128, chi)], axis=0)
    lines = [[4 * y + x for x in range(4)] for y in range(4)]
    gathered = lax.all_to_all(
        jnp.broadcast_to(own[None], (4, 384, chi)), "bond", 0, 0, axis_index_groups=lines, tiled=True
    )
    quarters = site[0].reshape(32, 4, 4, 128).transpose(2, 1, 0, 3)
    send = jnp.broadcast_to(quarters[None], (4, 4, 4, 32, 128)).reshape(16, 4, 32, 128)
    cols = lax.all_to_all(send, "bond", 0, 0, tiled=True)
    eye = jnp.eye(8, dtype=BF)
    kron = jnp.einsum("pq,mnsu->npuqsm", eye, mpo).reshape(256, 256)
    fresh = pl.pallas_call(
        front,
        out_shape=jax.ShapeDtypeStruct((16, 8, 32, 128), BF),
        in_specs=[VM] * 3,
        out_specs=VM,
        scratch_shapes=[pltpu.VMEM((128, 32, 128), BF), pltpu.VMEM((8, 512, 128), BF)],
        compiler_params=pltpu.CompilerParams(vmem_limit_bytes=40 << 20),
        cost_estimate=pl.CostEstimate(flops=2_000_000_000, bytes_accessed=4_000_000, transcendentals=0),
        name="front",
    )(gathered, cols, kron)
    fresh = lax.all_to_all(fresh, "bond", 0, 0, tiled=True).reshape(4, 4, 8, 32, 128).astype(F32)
    fresh = ((fresh[0] + fresh[1]) + (fresh[2] + fresh[3])).astype(BF)
    new_left = fresh.transpose(2, 1, 0, 3).reshape(32, 8, chi)
    source = shifted(new_left.reshape(256, chi), "sec", 1)
    two_site = jnp.einsum("mnsu,nkvw->kuwsvm", mpo, mpo, preferred_element_type=F32)
    two_site = two_site.astype(BF).reshape(128, 128)
    result = pl.pallas_call(
        back,
        grid=(8,),
        out_shape=jax.ShapeDtypeStruct((512, chi), BF),
        in_specs=[
            pl.BlockSpec((256, 512), lambda j: (0, 0)),
            pl.BlockSpec((512, 1024), lambda j: (0, j)),
            pl.BlockSpec((128, 128), lambda j: (0, 0)),
            pl.BlockSpec(memory_space=pl.ANY),
        ],
        out_specs=pl.BlockSpec((512, 512), lambda j: (0, 0)),
        scratch_shapes=[
            pltpu.VMEM((32, 128, 512), BF),
            pltpu.VMEM((512, 4096), BF),
            pltpu.VMEM((4096, 512), BF),
            pltpu.SemaphoreType.DMA,
        ],
        compiler_params=pltpu.CompilerParams(vmem_limit_bytes=58 << 20),
        cost_estimate=pl.CostEstimate(flops=5_000_000_000, bytes_accessed=14_000_000, transcendentals=0),
        name="back",
    )(source, pair, two_site, right_env[0].reshape(8 * chi, chi))
    return (new_left[None], result.reshape(1, 32, 4, 4, chi))


def solution(mesh):
    in_specs = (
        P("sec", "bond", None, None),
        P("sec", "bond", None, None),
        P("sec", "bond", None, None, None),
        P("sec", None, None, None),
        P(),
    )
    out_specs = (P("sec", "bond", None, None), P("sec", "bond", None, None, None))
    return jax.shard_map(shards, mesh=mesh, in_specs=in_specs, out_specs=out_specs, check_vma=False)
```

```python
import jax
import jax.numpy as jnp
from jax import lax
from jax.experimental import pallas as pl
from jax.experimental.pallas import tpu as pltpu
from jax.sharding import PartitionSpec as P

BF = jnp.bfloat16
F32 = jnp.float32
VM = pl.BlockSpec(memory_space=pltpu.VMEM)


LINE = 4


def line_route(distance):
    return [(i, i - i % LINE + (i + distance) % LINE) for i in range(LINE * LINE)]


def front(own, near, back_, far, cols, local, out, first, second):
    ket = jnp.concatenate([cols[:, s].reshape(512, 128) for s in range(4)], axis=1)
    blocks = (own, near, back_, far)
    for g, block in enumerate(blocks):
        f = jnp.dot(block[:256, :], ket, preferred_element_type=F32)
        for h in range(2):
            part = [f[:, 128 * s : 128 * s + 128].reshape(32, 8, 128) for s in (2 * h, 2 * h + 1)]
            first[32 * g : 32 * g + 32, 16 * h : 16 * h + 16, :] = jnp.concatenate(part, axis=1).astype(BF)
    row = lax.broadcasted_iota(jnp.int32, (256, 32), 0)
    col = lax.broadcasted_iota(jnp.int32, (256, 32), 1)
    spread = ((row >> 5) * 4 + (row & 3) == col).astype(BF)
    row = lax.broadcasted_iota(jnp.int32, (32, 256), 0)
    col = lax.broadcasted_iota(jnp.int32, (32, 256), 1)
    copies = (row == (col & 31)).astype(BF)
    kron = jnp.dot(spread, local[...], preferred_element_type=F32).astype(BF)
    kron = jnp.dot(kron, copies, preferred_element_type=F32)
    row = lax.broadcasted_iota(jnp.int32, (256, 256), 0)
    col = lax.broadcasted_iota(jnp.int32, (256, 256), 1)
    kron = jnp.where(((row >> 2) & 7) == (col >> 5), kron, 0.0).astype(BF)
    for blk in range(0, 16, 2):
        f = [first[8 * i : 8 * i + 8].reshape(256, 128) for i in (blk, blk + 1)]
        o = jnp.dot(kron, jnp.concatenate(f, axis=1), preferred_element_type=F32).astype(BF)
        for i in range(2):
            second[:, 32 * (blk + i) : 32 * (blk + i) + 32, :] = o[:, 128 * i : 128 * i + 128].reshape(8, 32, 128)
    site = jnp.concatenate([block[256:, :] for block in blocks], axis=0)
    for n in range(0, 8, 2):
        f = jnp.concatenate([second[n], second[n + 1]], axis=1)
        o = lax.dot_general(site, f, (((0,), (0,)), ((), ())), preferred_element_type=F32).astype(BF)
        for i in range(2):
            out[:, n + i] = o[:, 128 * i : 128 * i + 128].reshape(16, 32, 128)


def back(left, pair, mix, right, out, mixed, proj, env, sem):
    j = pl.program_id(0)
    fetch = pltpu.make_async_copy(right, env, sem)

    @pl.when(j == 0)
    def _():
        fetch.start()

    m = jnp.dot(left[...], pair[...], preferred_element_type=F32)
    for h in range(2):
        part = [m[:, 256 * i : 256 * i + 256].reshape(32, 8, 256) for i in (2 * h, 2 * h + 1)]
        at = pl.ds(pl.multiple_of(32 * j + 16 * h, 16), 16)
        mixed[:, at, :] = jnp.concatenate(part, axis=1).astype(BF)

    @pl.when(j == 3)
    def _():
        for p in range(32):
            o = jnp.dot(mix[...], mixed[p], preferred_element_type=F32).astype(BF)
            for k in range(8):
                proj[16 * p : 16 * p + 16, 256 * k : 256 * k + 256] = o[16 * k : 16 * k + 16, :]
        fetch.wait()
        out[...] = jnp.dot(proj[...], env[...], preferred_element_type=F32).astype(BF)


def applied(left, pair, mix, right):
    return pl.pallas_call(
        back,
        grid=(4,),
        out_shape=jax.ShapeDtypeStruct((512, 512), BF),
        in_specs=[
            pl.BlockSpec((256, 512), lambda j: (0, 0)),
            pl.BlockSpec((512, 1024), lambda j: (0, j)),
            pl.BlockSpec((128, 128), lambda j: (0, 0)),
            pl.BlockSpec(memory_space=pl.ANY),
        ],
        out_specs=pl.BlockSpec((512, 512), lambda j: (0, 0)),
        scratch_shapes=[
            pltpu.VMEM((32, 128, 256), BF),
            pltpu.VMEM((512, 2048), BF),
            pltpu.VMEM((2048, 512), BF),
            pltpu.SemaphoreType.DMA,
        ],
        compiler_params=pltpu.CompilerParams(vmem_limit_bytes=32 << 20),
        cost_estimate=pl.CostEstimate(flops=2_500_000_000, bytes_accessed=8_000_000, transcendentals=0),
        name="back",
    )(left, pair, mix, right)


def shards(left_env, site, psi, right_env, mpo):
    chi = site.shape[-1]
    lines = [[LINE * y + x for x in range(LINE)] for y in range(LINE)]
    columns = [[LINE * y + x for y in range(LINE)] for x in range(LINE)]
    halves = psi[0].reshape(32, 16, 2, 256).transpose(2, 0, 1, 3).reshape(2, 32, 4096)
    send = jnp.broadcast_to(halves[None], (2, 2, 32, 4096)).reshape(4, 32, 4096)
    pair = lax.all_to_all(send, "bond", 0, 0, axis_index_groups=lines, tiled=True)
    pair = lax.all_gather(pair.reshape(128, 4096), "bond", axis=0, axis_index_groups=columns, tiled=True)
    own = jnp.concatenate([left_env[0].reshape(256, chi), site[0].reshape(128, chi)], axis=0)
    blocks = [own] + [lax.ppermute(own, "bond", line_route(d)) for d in (1, -1, 2)]
    quarters = site[0].reshape(32, 4, 4, 128).transpose(2, 1, 0, 3)
    send = jnp.broadcast_to(quarters[None], (4, 4, 4, 32, 128)).reshape(16, 4, 32, 128)
    cols = lax.all_to_all(send, "bond", 0, 0, tiled=True)
    local = mpo.transpose(1, 3, 2, 0).reshape(32, 32)
    fresh = pl.pallas_call(
        front,
        out_shape=jax.ShapeDtypeStruct((16, 8, 32, 128), BF),
        in_specs=[VM] * 6,
        out_specs=VM,
        scratch_shapes=[pltpu.VMEM((128, 32, 128), BF), pltpu.VMEM((8, 512, 128), BF)],
        compiler_params=pltpu.CompilerParams(vmem_limit_bytes=32 << 20),
        cost_estimate=pl.CostEstimate(flops=2_000_000_000, bytes_accessed=4_000_000, transcendentals=0),
        name="front",
    )(*blocks, cols, local)
    fresh = lax.all_to_all(fresh, "bond", 0, 0, tiled=True).reshape(4, 4, 8, 32, 128).astype(F32)
    fresh = ((fresh[0] + fresh[1]) + (fresh[2] + fresh[3])).astype(BF)
    new_left = fresh.transpose(2, 1, 0, 3).reshape(32, 8, chi)
    source = new_left.reshape(256, chi)
    other = lax.ppermute(source, "bond", [(i, i ^ 1) for i in range(16)])
    two_site = jnp.einsum("mnsu,nkvw->kuwsvm", mpo, mpo, preferred_element_type=F32)
    two_site = two_site.astype(BF).reshape(128, 128)
    sections = lax.axis_size("sec")
    start = lax.axis_index("bond") % 2 * 256
    right = lax.dynamic_slice_in_dim(right_env[0], start, 256, 1).reshape(2048, chi)
    right = lax.ppermute(right, "sec", [((i + 1) % sections, i) for i in range(sections)])
    total = 0.0
    for flip, left in ((0, source), (1, other)):
        part = applied(left, pair, two_site, right)
        route = [(16 * s + b, (s + 1) % sections * 16 + (b ^ flip)) for s in range(sections) for b in range(16)]
        total = total + lax.ppermute(part, ("sec", "bond"), route).astype(F32)
    return (new_left[None], total.astype(BF).reshape(1, 32, 4, 4, chi))


def solution(mesh):
    in_specs = (
        P("sec", "bond", None, None),
        P("sec", "bond", None, None),
        P("sec", "bond", None, None, None),
        P("sec", None, None, None),
        P(),
    )
    out_specs = (P("sec", "bond", None, None), P("sec", "bond", None, None, None))
    return jax.shard_map(shards, mesh=mesh, in_specs=in_specs, out_specs=out_specs, check_vma=False)
```

```python
import jax
import jax.numpy as jnp
from jax import lax
from jax.experimental import pallas as pl
from jax.experimental.pallas import tpu as pltpu
from jax.sharding import PartitionSpec as P

BF = jnp.bfloat16
F32 = jnp.float32
VM = pl.BlockSpec(memory_space=pltpu.VMEM)


LINE = 4


def line_route(distance):
    return [(i, i - i % LINE + (i + distance) % LINE) for i in range(LINE * LINE)]


def column_route(distance):
    size = LINE * LINE
    return [(i, (i + LINE * distance) % size) for i in range(size)]


def front(own, near, back_, far, cols, local, out, first, second):
    ket = jnp.concatenate([cols[:, s].reshape(512, 128) for s in range(4)], axis=1)
    blocks = (own, near, back_, far)
    for g, block in enumerate(blocks):
        f = jnp.dot(block[:256, :], ket, preferred_element_type=F32)
        for h in range(2):
            part = [f[:, 128 * s : 128 * s + 128].reshape(32, 8, 128) for s in (2 * h, 2 * h + 1)]
            first[32 * g : 32 * g + 32, 16 * h : 16 * h + 16, :] = jnp.concatenate(part, axis=1).astype(BF)
    row = lax.broadcasted_iota(jnp.int32, (256, 32), 0)
    col = lax.broadcasted_iota(jnp.int32, (256, 32), 1)
    spread = ((row >> 5) * 4 + (row & 3) == col).astype(BF)
    row = lax.broadcasted_iota(jnp.int32, (32, 256), 0)
    col = lax.broadcasted_iota(jnp.int32, (32, 256), 1)
    copies = (row == (col & 31)).astype(BF)
    kron = jnp.dot(spread, local[...], preferred_element_type=F32).astype(BF)
    kron = jnp.dot(kron, copies, preferred_element_type=F32)
    row = lax.broadcasted_iota(jnp.int32, (256, 256), 0)
    col = lax.broadcasted_iota(jnp.int32, (256, 256), 1)
    kron = jnp.where(((row >> 2) & 7) == (col >> 5), kron, 0.0).astype(BF)
    for blk in range(0, 16, 2):
        f = [first[8 * i : 8 * i + 8].reshape(256, 128) for i in (blk, blk + 1)]
        o = jnp.dot(kron, jnp.concatenate(f, axis=1), preferred_element_type=F32).astype(BF)
        for i in range(2):
            second[:, 32 * (blk + i) : 32 * (blk + i) + 32, :] = o[:, 128 * i : 128 * i + 128].reshape(8, 32, 128)
    site = jnp.concatenate([block[256:, :] for block in blocks], axis=0)
    for n in range(0, 8, 2):
        f = jnp.concatenate([second[n], second[n + 1]], axis=1)
        o = lax.dot_general(site, f, (((0,), (0,)), ((), ())), preferred_element_type=F32).astype(BF)
        for i in range(2):
            out[:, n + i] = o[:, 128 * i : 128 * i + 128].reshape(16, 32, 128)


def back(offsets, left, own, up, down, far_a, far_b, mix, right, out, ket, mixed, proj, env, sem):
    j = pl.program_id(0)
    fetch = pltpu.make_async_copy(right, env, sem)

    @pl.when(j == 0)
    def _():
        fetch.start()
        for i in range(4):
            ket[:, 128 * i : 128 * i + 128] = left[:, pl.ds(pl.multiple_of(offsets[i], 128), 128)]

    pair = jnp.concatenate([own[...], up[...], down[...], far_a[...], far_b[...]], axis=0)
    m = jnp.dot(ket[...], pair, preferred_element_type=F32)
    for h in range(2):
        part = [m[:, 256 * i : 256 * i + 256].reshape(32, 8, 256) for i in (2 * h, 2 * h + 1)]
        at = pl.ds(pl.multiple_of(32 * j + 16 * h, 16), 16)
        mixed[:, at, :] = jnp.concatenate(part, axis=1).astype(BF)

    @pl.when(j == 3)
    def _():
        for p in range(32):
            o = jnp.dot(mix[...], mixed[p], preferred_element_type=F32).astype(BF)
            for k in range(8):
                proj[16 * p : 16 * p + 16, 256 * k : 256 * k + 256] = o[16 * k : 16 * k + 16, :]
        fetch.wait()
        out[...] = jnp.dot(proj[...], env[...], preferred_element_type=F32).astype(BF)


def applied(offsets, left, pieces, mix, right):
    return pl.pallas_call(
        back,
        grid=(4,),
        out_shape=jax.ShapeDtypeStruct((512, 512), BF),
        in_specs=[
            pl.BlockSpec(memory_space=pltpu.SMEM),
            pl.BlockSpec((256, 512), lambda j: (0, 0)),
            *[pl.BlockSpec((p.shape[0], 1024), lambda j: (0, j)) for p in pieces],
            pl.BlockSpec((128, 128), lambda j: (0, 0)),
            pl.BlockSpec(memory_space=pl.ANY),
        ],
        out_specs=pl.BlockSpec((512, 512), lambda j: (0, 0)),
        scratch_shapes=[
            pltpu.VMEM((256, 512), BF),
            pltpu.VMEM((32, 128, 256), BF),
            pltpu.VMEM((512, 2048), BF),
            pltpu.VMEM((2048, 512), BF),
            pltpu.SemaphoreType.DMA,
        ],
        compiler_params=pltpu.CompilerParams(vmem_limit_bytes=32 << 20),
        cost_estimate=pl.CostEstimate(flops=2_500_000_000, bytes_accessed=8_000_000, transcendentals=0),
        name="back",
    )(offsets, left, *pieces, mix, right)


def shards(left_env, site, psi, right_env, mpo):
    chi = site.shape[-1]
    lines = [[LINE * y + x for x in range(LINE)] for y in range(LINE)]
    halves = psi[0].reshape(32, 16, 2, 256).transpose(2, 0, 1, 3).reshape(2, 32, 4096)
    send = jnp.broadcast_to(halves[None], (2, 2, 32, 4096)).reshape(4, 32, 4096)
    pair = lax.all_to_all(send, "bond", 0, 0, axis_index_groups=lines, tiled=True)
    pair = pair.reshape(128, 4096)
    up = lax.ppermute(pair, "bond", column_route(1))
    down = lax.ppermute(pair, "bond", column_route(-1))
    far_a = lax.ppermute(up[:64], "bond", column_route(1))
    far_b = lax.ppermute(down[64:], "bond", column_route(-1))
    pieces = (pair, up, down, far_a, far_b)
    offsets = (lax.axis_index("bond") // LINE + jnp.array([0, 3, 1, 2], jnp.int32)) % LINE * 128
    own = jnp.concatenate([left_env[0].reshape(256, chi), site[0].reshape(128, chi)], axis=0)
    blocks = [own] + [lax.ppermute(own, "bond", line_route(d)) for d in (1, -1, 2)]
    quarters = site[0].reshape(32, 4, 4, 128).transpose(2, 1, 0, 3)
    send = jnp.broadcast_to(quarters[None], (4, 4, 4, 32, 128)).reshape(16, 4, 32, 128)
    cols = lax.all_to_all(send, "bond", 0, 0, tiled=True)
    local = mpo.transpose(1, 3, 2, 0).reshape(32, 32)
    fresh = pl.pallas_call(
        front,
        out_shape=jax.ShapeDtypeStruct((16, 8, 32, 128), BF),
        in_specs=[VM] * 6,
        out_specs=VM,
        scratch_shapes=[pltpu.VMEM((128, 32, 128), BF), pltpu.VMEM((8, 512, 128), BF)],
        compiler_params=pltpu.CompilerParams(vmem_limit_bytes=32 << 20),
        cost_estimate=pl.CostEstimate(flops=2_000_000_000, bytes_accessed=4_000_000, transcendentals=0),
        name="front",
    )(*blocks, cols, local)
    fresh = lax.all_to_all(fresh, "bond", 0, 0, tiled=True).reshape(4, 4, 8, 32, 128).astype(F32)
    fresh = ((fresh[0] + fresh[1]) + (fresh[2] + fresh[3])).astype(BF)
    new_left = fresh.transpose(2, 1, 0, 3).reshape(32, 8, chi)
    source = new_left.reshape(256, chi)
    other = lax.ppermute(source, "bond", [(i, i ^ 1) for i in range(16)])
    two_site = jnp.einsum("mnsu,nkvw->kuwsvm", mpo, mpo, preferred_element_type=F32)
    two_site = two_site.astype(BF).reshape(128, 128)
    sections = lax.axis_size("sec")
    start = lax.axis_index("bond") % 2 * 256
    right = lax.dynamic_slice_in_dim(right_env[0], start, 256, 1).reshape(2048, chi)
    right = lax.ppermute(right, "sec", [((i + 1) % sections, i) for i in range(sections)])
    total = 0.0
    for flip, left in ((0, source), (1, other)):
        part = applied(offsets, left, pieces, two_site, right)
        route = [(16 * s + b, (s + 1) % sections * 16 + (b ^ flip)) for s in range(sections) for b in range(16)]
        total = total + lax.ppermute(part, ("sec", "bond"), route).astype(F32)
    return (new_left[None], total.astype(BF).reshape(1, 32, 4, 4, chi))


def solution(mesh):
    in_specs = (
        P("sec", "bond", None, None),
        P("sec", "bond", None, None),
        P("sec", "bond", None, None, None),
        P("sec", None, None, None),
        P(),
    )
    out_specs = (P("sec", "bond", None, None), P("sec", "bond", None, None, None))
    return jax.shard_map(shards, mesh=mesh, in_specs=in_specs, out_specs=out_specs, check_vma=False)
```

```python
import jax
import jax.numpy as jnp
from jax import lax
from jax.experimental import pallas as pl
from jax.experimental.pallas import tpu as pltpu
from jax.sharding import PartitionSpec as P

BF = jnp.bfloat16
F32 = jnp.float32
VM = pl.BlockSpec(memory_space=pltpu.VMEM)


LINE = 4


def line_route(distance):
    return [(i, i - i % LINE + (i + distance) % LINE) for i in range(LINE * LINE)]


def column_route(distance):
    size = LINE * LINE
    return [(i, (i + LINE * distance) % size) for i in range(size)]


def spread_out(local):
    row = lax.broadcasted_iota(jnp.int32, (256, 32), 0)
    col = lax.broadcasted_iota(jnp.int32, (256, 32), 1)
    spread = ((row >> 5) * 4 + (row & 3) == col).astype(BF)
    row = lax.broadcasted_iota(jnp.int32, (32, 256), 0)
    col = lax.broadcasted_iota(jnp.int32, (32, 256), 1)
    copies = (row == (col & 31)).astype(BF)
    kron = jnp.dot(spread, local[...], preferred_element_type=F32).astype(BF)
    kron = jnp.dot(kron, copies, preferred_element_type=F32)
    row = lax.broadcasted_iota(jnp.int32, (256, 256), 0)
    col = lax.broadcasted_iota(jnp.int32, (256, 256), 1)
    kron = jnp.where(((row >> 2) & 7) == (col >> 5), kron, 0.0).astype(BF)
    return kron


def front(own, near, back_, far, cols, local, out, first, second, held, heldc, sems):
    fetches = [pltpu.make_async_copy(ref, held.at[i], sems.at[i]) for i, ref in enumerate((own, near, back_, far))]
    fetches = [pltpu.make_async_copy(cols, heldc, sems.at[4])] + fetches
    for fetch in fetches:
        fetch.start()
    kron = spread_out(local)
    fetches[0].wait()
    cols = heldc
    ket = jnp.concatenate([cols[:, s].reshape(512, 128) for s in range(4)], axis=1)
    for g in range(4):
        fetches[1 + g].wait()
        block = held[g]
        f = jnp.dot(block[:256, :], ket, preferred_element_type=F32)
        for h in range(2):
            part = [f[:, 128 * s : 128 * s + 128].reshape(32, 8, 128) for s in (2 * h, 2 * h + 1)]
            first[32 * g : 32 * g + 32, 16 * h : 16 * h + 16, :] = jnp.concatenate(part, axis=1).astype(BF)
    for blk in range(0, 16, 2):
        f = [first[8 * i : 8 * i + 8].reshape(256, 128) for i in (blk, blk + 1)]
        o = jnp.dot(kron, jnp.concatenate(f, axis=1), preferred_element_type=F32).astype(BF)
        for i in range(2):
            second[:, 32 * (blk + i) : 32 * (blk + i) + 32, :] = o[:, 128 * i : 128 * i + 128].reshape(8, 32, 128)
    site = held[:, 256:, :].reshape(512, 512)
    for n in range(0, 8, 2):
        f = jnp.concatenate([second[n], second[n + 1]], axis=1)
        o = lax.dot_general(site, f, (((0,), (0,)), ((), ())), preferred_element_type=F32).astype(BF)
        for i in range(2):
            out[:, n + i] = o[:, 128 * i : 128 * i + 128].reshape(16, 32, 128)


def back(offsets, left, own, up, down, far_a, far_b, mix, right, out, mixed, proj):
    ket = [left[:, pl.ds(pl.multiple_of(offsets[i], 128), 128)] for i in range(4)]
    ket = jnp.concatenate(ket, axis=1)
    for h in range(8):
        at = slice(512 * h, 512 * h + 512)
        pair = jnp.concatenate([ref[:, at] for ref in (own, up, down, far_a, far_b)], axis=0)
        m = jnp.dot(ket, pair, preferred_element_type=F32)
        part = [m[:, 256 * i : 256 * i + 256].reshape(32, 8, 256) for i in range(2)]
        mixed[:, 16 * h : 16 * h + 16, :] = jnp.concatenate(part, axis=1).astype(BF)
    for p in range(32):
        o = jnp.dot(mix[...], mixed[p], preferred_element_type=F32).astype(BF)
        for k in range(8):
            proj[16 * p : 16 * p + 16, 256 * k : 256 * k + 256] = o[16 * k : 16 * k + 16, :]
    out[...] = jnp.dot(proj[...], right[...], preferred_element_type=F32).astype(BF)


def applied(offsets, left, pieces, mix, right):
    return pl.pallas_call(
        back,
        out_shape=jax.ShapeDtypeStruct((512, 512), BF),
        in_specs=[pl.BlockSpec(memory_space=pltpu.SMEM)] + [VM] * 8,
        out_specs=VM,
        scratch_shapes=[pltpu.VMEM((32, 128, 256), BF), pltpu.VMEM((512, 2048), BF)],
        compiler_params=pltpu.CompilerParams(vmem_limit_bytes=24 << 20),
        cost_estimate=pl.CostEstimate(flops=2_500_000_000, bytes_accessed=8_000_000, transcendentals=0),
        name="back",
    )(offsets, left, *pieces, mix, right)


def shards(left_env, site, psi, right_env, mpo):
    chi = site.shape[-1]
    sections = lax.axis_size("sec")
    here = lax.axis_index("bond")
    lines = [[LINE * y + x for x in range(LINE)] for y in range(LINE)]

    def next_section(block, flip):
        route = [(16 * s + b, (s + 1) % sections * 16 + (b ^ flip)) for s in range(sections) for b in range(16)]
        return lax.ppermute(block, ("sec", "bond"), route)

    own = jnp.concatenate([left_env[0].reshape(256, chi), site[0].reshape(128, chi)], axis=0)
    blocks = [own] + [lax.ppermute(own, "bond", line_route(d)) for d in (1, -1, 2)]
    pair = next_section(psi[0], 0)
    halves = pair.reshape(32, 16, 2, 256).transpose(2, 0, 1, 3).reshape(2, 32, 4096)
    send = jnp.broadcast_to(halves[None], (2, 2, 32, 4096)).reshape(4, 32, 4096)
    pair = lax.all_to_all(send, "bond", 0, 0, axis_index_groups=lines, tiled=True).reshape(128, 4096)
    local = mpo.transpose(1, 3, 2, 0).reshape(32, 32)
    two_site = jnp.einsum("mnsu,nkvw->kuwsvm", mpo, mpo, preferred_element_type=F32)
    two_site = two_site.astype(BF).reshape(128, 128)
    quarters = site[0].reshape(32, 4, 4, 128).transpose(2, 1, 0, 3)
    cols = jnp.broadcast_to(quarters[None], (4, 4, 4, 32, 128)).reshape(16, 4, 32, 128)
    offsets = (here // LINE + jnp.array([0, 3, 1, 2], jnp.int32)) % LINE * 128
    right = lax.dynamic_slice_in_dim(right_env[0], here % 2 * 256, 256, 1).reshape(2048, chi)
    pair, local, two_site, cols, offsets, right = lax.optimization_barrier(
        (pair, local, two_site, cols, offsets, right)
    )
    up = lax.ppermute(pair, "bond", column_route(1))
    down = lax.ppermute(pair, "bond", column_route(-1))
    far_a = lax.ppermute(up[:64], "bond", column_route(1))
    far_b = lax.ppermute(down[64:], "bond", column_route(-1))
    pieces = (pair, up, down, far_a, far_b)
    cols = lax.all_to_all(cols, "bond", 0, 0, tiled=True)
    fresh = pl.pallas_call(
        front,
        out_shape=jax.ShapeDtypeStruct((16, 8, 32, 128), BF),
        in_specs=[pl.BlockSpec(memory_space=pl.ANY)] * 5 + [VM],
        out_specs=VM,
        scratch_shapes=[
            pltpu.VMEM((128, 32, 128), BF),
            pltpu.VMEM((8, 512, 128), BF),
            pltpu.VMEM((4, 384, 512), BF),
            pltpu.VMEM((16, 4, 32, 128), BF),
            pltpu.SemaphoreType.DMA((5,)),
        ],
        compiler_params=pltpu.CompilerParams(vmem_limit_bytes=56 << 20),
        cost_estimate=pl.CostEstimate(flops=2_000_000_000, bytes_accessed=4_000_000, transcendentals=0),
        name="front",
    )(*blocks, cols, local)
    fresh = lax.all_to_all(fresh, "bond", 0, 0, tiled=True).reshape(4, 4, 8, 32, 128)
    fresh = [fresh[i].astype(F32) for i in range(4)]
    fresh = ((fresh[0] + fresh[1]) + (fresh[2] + fresh[3])).astype(BF)
    new_left = fresh.transpose(2, 1, 0, 3).reshape(32, 8, chi)
    source = new_left.reshape(256, chi)
    other = next_section(source, 1)
    source = next_section(source, 0)
    give = applied(offsets, other, pieces, two_site, right)
    source, give = lax.optimization_barrier((source, give))
    take = lax.ppermute(give, "bond", [(i, i ^ 1) for i in range(16)])
    keep = applied(offsets, source, pieces, two_site, right)
    total = (keep.astype(F32) + take.astype(F32)).astype(BF)
    return (new_left[None], total.reshape(1, 32, 4, 4, chi))


def solution(mesh):
    in_specs = (
        P("sec", "bond", None, None),
        P("sec", "bond", None, None),
        P("sec", "bond", None, None, None),
        P("sec", None, None, None),
        P(),
    )
    out_specs = (P("sec", "bond", None, None), P("sec", "bond", None, None, None))
    return jax.shard_map(shards, mesh=mesh, in_specs=in_specs, out_specs=out_specs, check_vma=False)
```

```python
import jax
import jax.numpy as jnp
from jax import lax
from jax.experimental import pallas as pl
from jax.experimental.pallas import tpu as pltpu
from jax.sharding import PartitionSpec as P

BF = jnp.bfloat16
F32 = jnp.float32
VM = pl.BlockSpec(memory_space=pltpu.VMEM)


LINE = 4
SIZE = LINE * LINE


def turned(b):
    return b % LINE * LINE + b // LINE


def routed(sections, step, ahead=0):
    pairs = []
    for s in range(sections):
        t = (s + ahead) % sections
        for b in range(SIZE):
            pairs.append((SIZE * s + b, SIZE * t + (turned(step(turned(b))) if t % 2 else step(b))))
    return pairs


def along_line(distance):
    return lambda b: b - b % LINE + (b + distance) % LINE


def along_column(distance):
    return lambda b: (b + LINE * distance) % SIZE


def spread_out(local):
    row = lax.broadcasted_iota(jnp.int32, (256, 32), 0)
    col = lax.broadcasted_iota(jnp.int32, (256, 32), 1)
    spread = ((row >> 5) * 4 + (row & 3) == col).astype(BF)
    row = lax.broadcasted_iota(jnp.int32, (32, 256), 0)
    col = lax.broadcasted_iota(jnp.int32, (32, 256), 1)
    copies = (row == (col & 31)).astype(BF)
    kron = jnp.dot(spread, local[...], preferred_element_type=F32).astype(BF)
    kron = jnp.dot(kron, copies, preferred_element_type=F32)
    row = lax.broadcasted_iota(jnp.int32, (256, 256), 0)
    col = lax.broadcasted_iota(jnp.int32, (256, 256), 1)
    kron = jnp.where(((row >> 2) & 7) == (col >> 5), kron, 0.0).astype(BF)
    return kron


def front(own, near, back_, far, cols, local, out, first, second, held, heldc, sems):
    fetches = [pltpu.make_async_copy(ref, held.at[i], sems.at[i]) for i, ref in enumerate((own, near, back_, far))]
    fetches = [pltpu.make_async_copy(cols, heldc, sems.at[4])] + fetches
    for fetch in fetches:
        fetch.start()
    kron = spread_out(local)
    fetches[0].wait()
    cols = heldc
    ket = jnp.concatenate([cols[:, s].reshape(512, 128) for s in range(4)], axis=1)
    for g in range(4):
        fetches[1 + g].wait()
        block = held[g]
        f = jnp.dot(block[:256, :], ket, preferred_element_type=F32)
        for h in range(2):
            part = [f[:, 128 * s : 128 * s + 128].reshape(32, 8, 128) for s in (2 * h, 2 * h + 1)]
            first[32 * g : 32 * g + 32, 16 * h : 16 * h + 16, :] = jnp.concatenate(part, axis=1).astype(BF)
    for blk in range(0, 16, 2):
        f = [first[8 * i : 8 * i + 8].reshape(256, 128) for i in (blk, blk + 1)]
        o = jnp.dot(kron, jnp.concatenate(f, axis=1), preferred_element_type=F32).astype(BF)
        for i in range(2):
            second[:, 32 * (blk + i) : 32 * (blk + i) + 32, :] = o[:, 128 * i : 128 * i + 128].reshape(8, 32, 128)
    site = held[:, 256:, :].reshape(512, 512)
    for n in range(0, 8, 2):
        f = jnp.concatenate([second[n], second[n + 1]], axis=1)
        o = lax.dot_general(site, f, (((0,), (0,)), ((), ())), preferred_element_type=F32).astype(BF)
        for i in range(2):
            out[:, n + i] = o[:, 128 * i : 128 * i + 128].reshape(16, 32, 128)


def back(offsets, left, own, up, down, far_a, far_b, mix, right, out, mixed, proj):
    ket = [left[:, pl.ds(pl.multiple_of(offsets[i], 128), 128)] for i in range(4)]
    ket = jnp.concatenate(ket, axis=1)
    for h in range(8):
        at = slice(512 * h, 512 * h + 512)
        pair = jnp.concatenate([ref[:, at] for ref in (own, up, down, far_a, far_b)], axis=0)
        m = jnp.dot(ket, pair, preferred_element_type=F32)
        part = [m[:, 256 * i : 256 * i + 256].reshape(32, 8, 256) for i in range(2)]
        mixed[:, 16 * h : 16 * h + 16, :] = jnp.concatenate(part, axis=1).astype(BF)
    for p in range(32):
        o = jnp.dot(mix[...], mixed[p], preferred_element_type=F32).astype(BF)
        for k in range(8):
            proj[16 * p : 16 * p + 16, 256 * k : 256 * k + 256] = o[16 * k : 16 * k + 16, :]
    out[...] = jnp.dot(proj[...], right[...], preferred_element_type=F32).astype(BF)


def applied(offsets, left, pieces, mix, right):
    return pl.pallas_call(
        back,
        out_shape=jax.ShapeDtypeStruct((512, 512), BF),
        in_specs=[pl.BlockSpec(memory_space=pltpu.SMEM)] + [VM] * 8,
        out_specs=VM,
        scratch_shapes=[pltpu.VMEM((32, 128, 256), BF), pltpu.VMEM((512, 2048), BF)],
        compiler_params=pltpu.CompilerParams(vmem_limit_bytes=24 << 20),
        cost_estimate=pl.CostEstimate(flops=2_500_000_000, bytes_accessed=8_000_000, transcendentals=0),
        name="back",
    )(offsets, left, *pieces, mix, right)


def shards(left_env, site, psi, right_env, mpo):
    chi = site.shape[-1]
    sections = lax.axis_size("sec")
    here = lax.axis_index("bond")
    odd = lax.axis_index("sec") % 2 == 1
    row = jnp.where(odd, here % LINE, here // LINE)
    column = jnp.where(odd, here // LINE, here % LINE)

    def moved(block, step, ahead=0):
        return lax.ppermute(block, ("sec", "bond"), routed(sections, step, ahead))

    lines = []
    for s in range(sections):
        for y in range(LINE):
            line = [LINE * y + x for x in range(LINE)]
            lines.append([SIZE * s + (turned(b) if s % 2 else b) for b in line])
    own = jnp.concatenate([left_env[0].reshape(256, chi), site[0].reshape(128, chi)], axis=0)
    blocks = [own] + [moved(own, along_line(d)) for d in (1, -1, 2)]
    pair = moved(psi[0], lambda b: b, 1)
    halves = pair.reshape(32, 16, 2, 256).transpose(2, 0, 1, 3).reshape(2, 32, 4096)
    send = jnp.broadcast_to(halves[None], (2, 2, 32, 4096)).reshape(4, 32, 4096)
    pair = lax.all_to_all(send, ("sec", "bond"), 0, 0, axis_index_groups=lines, tiled=True).reshape(128, 4096)
    local = mpo.transpose(1, 3, 2, 0).reshape(32, 32)
    two_site = jnp.einsum("mnsu,nkvw->kuwsvm", mpo, mpo, preferred_element_type=F32)
    two_site = two_site.astype(BF).reshape(128, 128)
    turn = site[0].reshape(32, 4, 4, 4, 32).transpose(0, 1, 3, 2, 4).reshape(32, 4, chi)
    tensor = jnp.where(odd, site[0], turn)
    quarters = tensor.reshape(32, 4, 4, 128).transpose(2, 1, 0, 3)
    cols = jnp.where(odd, quarters[:, None], quarters[None]).reshape(16, 4, 32, 128)
    offsets = (row + jnp.array([0, 3, 1, 2], jnp.int32)) % LINE * 128
    right = lax.dynamic_slice_in_dim(right_env[0], column % 2 * 256, 256, 1).reshape(2048, chi)
    pair, local, two_site, cols, offsets, right = lax.optimization_barrier(
        (pair, local, two_site, cols, offsets, right)
    )
    up = moved(pair, along_column(1))
    down = moved(pair, along_column(-1))
    far_a = moved(up[:64], along_column(1))
    far_b = moved(down[64:], along_column(-1))
    pieces = (pair, up, down, far_a, far_b)
    cols = lax.all_to_all(cols, "bond", 0, 0, tiled=True)
    fresh = pl.pallas_call(
        front,
        out_shape=jax.ShapeDtypeStruct((16, 8, 32, 128), BF),
        in_specs=[pl.BlockSpec(memory_space=pl.ANY)] * 5 + [VM],
        out_specs=VM,
        scratch_shapes=[
            pltpu.VMEM((128, 32, 128), BF),
            pltpu.VMEM((8, 512, 128), BF),
            pltpu.VMEM((4, 384, 512), BF),
            pltpu.VMEM((16, 4, 32, 128), BF),
            pltpu.SemaphoreType.DMA((5,)),
        ],
        compiler_params=pltpu.CompilerParams(vmem_limit_bytes=56 << 20),
        cost_estimate=pl.CostEstimate(flops=2_000_000_000, bytes_accessed=4_000_000, transcendentals=0),
        name="front",
    )(*blocks, cols, local)
    fresh = lax.all_to_all(fresh, "bond", 0, 0, tiled=True).reshape(4, 4, 8, 32, 128)
    fresh = jnp.where(odd, fresh.transpose(1, 0, 2, 3, 4), fresh)
    fresh = [fresh[i].astype(F32) for i in range(4)]
    fresh = ((fresh[0] + fresh[1]) + (fresh[2] + fresh[3])).astype(BF)
    source = fresh.transpose(2, 1, 0, 3).reshape(256, chi)
    new_left = source.reshape(32, 8, chi)
    turn = new_left.reshape(32, 8, 4, 4, 32).transpose(0, 1, 3, 2, 4).reshape(32, 8, chi)
    new_left = jnp.where(odd, new_left, turn)
    other = moved(source, lambda b: b ^ 1, 1)
    source = moved(source, lambda b: b, 1)
    give = applied(offsets, other, pieces, two_site, right)
    source, give = lax.optimization_barrier((source, give))
    take = moved(give, lambda b: b ^ 1)
    keep = applied(offsets, source, pieces, two_site, right)
    total = (keep.astype(F32) + take.astype(F32)).astype(BF)
    return (new_left[None], total.reshape(1, 32, 4, 4, chi))


def solution(mesh):
    in_specs = (
        P("sec", "bond", None, None),
        P("sec", "bond", None, None),
        P("sec", "bond", None, None, None),
        P("sec", None, None, None),
        P(),
    )
    out_specs = (P("sec", "bond", None, None), P("sec", "bond", None, None, None))
    return jax.shard_map(shards, mesh=mesh, in_specs=in_specs, out_specs=out_specs, check_vma=False)
```

```python
import jax
import jax.numpy as jnp
from jax import lax
from jax.experimental import pallas as pl
from jax.experimental.pallas import tpu as pltpu
from jax.sharding import PartitionSpec as P

BF = jnp.bfloat16
F32 = jnp.float32
VM = pl.BlockSpec(memory_space=pltpu.VMEM)


LINE = 4
SIZE = LINE * LINE


def turned(b):
    return b % LINE * LINE + b // LINE


def routed(sections, step, ahead=0):
    pairs = []
    for s in range(sections):
        t = (s + ahead) % sections
        for b in range(SIZE):
            pairs.append((SIZE * s + b, SIZE * t + (turned(step(turned(b))) if t % 2 else step(b))))
    return pairs


def along_line(distance):
    return lambda b: b - b % LINE + (b + distance) % LINE


def along_column(distance):
    return lambda b: (b + LINE * distance) % SIZE


def spread_out(local):
    row = lax.broadcasted_iota(jnp.int32, (256, 32), 0)
    col = lax.broadcasted_iota(jnp.int32, (256, 32), 1)
    spread = ((row >> 5) * 4 + (row & 3) == col).astype(BF)
    row = lax.broadcasted_iota(jnp.int32, (32, 256), 0)
    col = lax.broadcasted_iota(jnp.int32, (32, 256), 1)
    copies = (row == (col & 31)).astype(BF)
    kron = jnp.dot(spread, local[...], preferred_element_type=F32).astype(BF)
    kron = jnp.dot(kron, copies, preferred_element_type=F32)
    row = lax.broadcasted_iota(jnp.int32, (256, 256), 0)
    col = lax.broadcasted_iota(jnp.int32, (256, 256), 1)
    kron = jnp.where(((row >> 2) & 7) == (col >> 5), kron, 0.0).astype(BF)
    return kron


def front(own, near, back_, far, cols, local, out, first, second, held, heldc, sems):
    fetches = [pltpu.make_async_copy(ref, held.at[i], sems.at[i]) for i, ref in enumerate((own, near, back_, far))]
    fetches = [pltpu.make_async_copy(cols, heldc, sems.at[4])] + fetches
    for fetch in fetches:
        fetch.start()
    kron = spread_out(local)
    fetches[0].wait()
    cols = heldc
    ket = jnp.concatenate([cols[:, s].reshape(512, 128) for s in range(4)], axis=1)
    for g in range(4):
        fetches[1 + g].wait()
        block = held[g]
        f = jnp.dot(block[:256, :], ket, preferred_element_type=F32)
        for h in range(2):
            part = [f[:, 128 * s : 128 * s + 128].reshape(32, 8, 128) for s in (2 * h, 2 * h + 1)]
            first[32 * g : 32 * g + 32, 16 * h : 16 * h + 16, :] = jnp.concatenate(part, axis=1).astype(BF)
    for blk in range(0, 16, 2):
        f = [first[8 * i : 8 * i + 8].reshape(256, 128) for i in (blk, blk + 1)]
        o = jnp.dot(kron, jnp.concatenate(f, axis=1), preferred_element_type=F32).astype(BF)
        for i in range(2):
            second[:, 32 * (blk + i) : 32 * (blk + i) + 32, :] = o[:, 128 * i : 128 * i + 128].reshape(8, 32, 128)
    site = held[:, 256:, :].reshape(512, 512)
    for n in range(0, 8, 2):
        f = jnp.concatenate([second[n], second[n + 1]], axis=1)
        o = lax.dot_general(site, f, (((0,), (0,)), ((), ())), preferred_element_type=F32).astype(BF)
        for i in range(2):
            out[:, n + i] = o[:, 128 * i : 128 * i + 128].reshape(16, 32, 128)


def back(offsets, left, own, up, down, far_a, far_b, mix, right, out, mixed, proj):
    ket = [left[:, pl.ds(pl.multiple_of(offsets[i], 128), 128)] for i in range(4)]
    ket = jnp.concatenate(ket, axis=1)
    for h in range(8):
        at = slice(512 * h, 512 * h + 512)
        pair = jnp.concatenate([ref[:, at] for ref in (own, up, down, far_a, far_b)], axis=0)
        m = jnp.dot(ket, pair, preferred_element_type=F32)
        part = [m[:, 256 * i : 256 * i + 256].reshape(32, 8, 256) for i in range(2)]
        mixed[:, 16 * h : 16 * h + 16, :] = jnp.concatenate(part, axis=1).astype(BF)
    for p in range(32):
        o = jnp.dot(mix[...], mixed[p], preferred_element_type=F32).astype(BF)
        for k in range(8):
            proj[16 * p : 16 * p + 16, 256 * k : 256 * k + 256] = o[16 * k : 16 * k + 16, :]
    out[...] = jnp.dot(proj[...], right[...], preferred_element_type=F32).astype(BF)


def applied(offsets, left, pieces, mix, right):
    return pl.pallas_call(
        back,
        out_shape=jax.ShapeDtypeStruct((512, 512), BF),
        in_specs=[pl.BlockSpec(memory_space=pltpu.SMEM)] + [VM] * 8,
        out_specs=VM,
        scratch_shapes=[pltpu.VMEM((32, 128, 256), BF), pltpu.VMEM((512, 2048), BF)],
        compiler_params=pltpu.CompilerParams(vmem_limit_bytes=24 << 20),
        cost_estimate=pl.CostEstimate(flops=2_500_000_000, bytes_accessed=8_000_000, transcendentals=0),
        name="back",
    )(offsets, left, *pieces, mix, right)


def shards(left_env, site, psi, right_env, mpo):
    chi = site.shape[-1]
    sections = lax.axis_size("sec")
    here = lax.axis_index("bond")
    odd = lax.axis_index("sec") % 2 == 1
    row = jnp.where(odd, here % LINE, here // LINE)
    column = jnp.where(odd, here // LINE, here % LINE)

    def moved(block, step, ahead=0):
        return lax.ppermute(block, ("sec", "bond"), routed(sections, step, ahead))

    lines = []
    for s in range(sections):
        for y in range(LINE):
            line = [LINE * y + x for x in range(LINE)]
            lines.append([SIZE * s + (turned(b) if s % 2 else b) for b in line])
    own = jnp.concatenate([left_env[0].reshape(256, chi), site[0].reshape(128, chi)], axis=0)
    blocks = [own] + [moved(own, along_line(d)) for d in (1, -1, 2)]
    pair = moved(psi[0], lambda b: b, 1)
    halves = pair.reshape(32, 16, 2, 256).transpose(2, 0, 1, 3).reshape(2, 32, 4096)
    send = jnp.broadcast_to(halves[None], (2, 2, 32, 4096)).reshape(4, 32, 4096)
    pair = lax.all_to_all(send, ("sec", "bond"), 0, 0, axis_index_groups=lines, tiled=True).reshape(128, 4096)
    local = mpo.transpose(1, 3, 2, 0).reshape(32, 32)
    two_site = jnp.einsum("mnsu,nkvw->kuwsvm", mpo, mpo, preferred_element_type=F32)
    two_site = two_site.astype(BF).reshape(128, 128)
    turn = site[0].reshape(32, 4, 4, 4, 32).transpose(0, 1, 3, 2, 4).reshape(32, 4, chi)
    tensor = jnp.where(odd, site[0], turn)
    quarters = tensor.reshape(32, 4, 4, 128).transpose(2, 1, 0, 3)
    cols = jnp.where(odd, quarters[:, None], quarters[None]).reshape(16, 4, 32, 128)
    offsets = (row + jnp.array([0, 3, 1, 2], jnp.int32)) % LINE * 128
    right = lax.dynamic_slice_in_dim(right_env[0], column % 2 * 256, 256, 1).reshape(2048, chi)
    pair, local, two_site, cols, offsets, right = lax.optimization_barrier(
        (pair, local, two_site, cols, offsets, right)
    )
    up = moved(pair, along_column(1))
    down = moved(pair, along_column(-1))
    far_a = moved(up[:64], along_column(1))
    far_b = moved(down[64:], along_column(-1))
    pieces = (pair, up, down, far_a, far_b)
    cols = lax.all_to_all(cols, "bond", 0, 0, tiled=True)
    fresh = pl.pallas_call(
        front,
        out_shape=jax.ShapeDtypeStruct((16, 8, 32, 128), BF),
        in_specs=[pl.BlockSpec(memory_space=pl.ANY)] * 5 + [VM],
        out_specs=VM,
        scratch_shapes=[
            pltpu.VMEM((128, 32, 128), BF),
            pltpu.VMEM((8, 512, 128), BF),
            pltpu.VMEM((4, 384, 512), BF),
            pltpu.VMEM((16, 4, 32, 128), BF),
            pltpu.SemaphoreType.DMA((5,)),
        ],
        compiler_params=pltpu.CompilerParams(vmem_limit_bytes=56 << 20),
        cost_estimate=pl.CostEstimate(flops=2_000_000_000, bytes_accessed=4_000_000, transcendentals=0),
        name="front",
    )(*blocks, cols, local)
    fresh = lax.all_to_all(fresh, "bond", 0, 0, tiled=True).reshape(4, 4, 8, 32, 128)
    fresh = jnp.where(odd, fresh.transpose(1, 0, 2, 3, 4), fresh)
    fresh = [fresh[i].astype(F32) for i in range(4)]
    fresh = ((fresh[0] + fresh[1]) + (fresh[2] + fresh[3])).astype(BF)
    source = fresh.transpose(2, 1, 0, 3).reshape(256, chi)
    i = lax.broadcasted_iota(jnp.int32, (chi, chi), 0)
    j = lax.broadcasted_iota(jnp.int32, (chi, chi), 1)
    place = jnp.where(odd, i, i // 32 % 4 * 128 + i // 128 * 32 + i % 32)
    place = (place == j).astype(BF)
    source, place = lax.optimization_barrier((source, place))
    new_left = jnp.dot(source, place, preferred_element_type=F32).astype(BF).reshape(32, 8, chi)
    other = moved(source, lambda b: b ^ 1, 1)
    source = moved(source, lambda b: b, 1)
    give = applied(offsets, other, pieces, two_site, right)
    source, give = lax.optimization_barrier((source, give))
    take = moved(give, lambda b: b ^ 1)
    keep = applied(offsets, source, pieces, two_site, right)
    total = (keep.astype(F32) + take.astype(F32)).astype(BF)
    return (new_left[None], total.reshape(1, 32, 4, 4, chi))


def solution(mesh):
    in_specs = (
        P("sec", "bond", None, None),
        P("sec", "bond", None, None),
        P("sec", "bond", None, None, None),
        P("sec", None, None, None),
        P(),
    )
    out_specs = (P("sec", "bond", None, None), P("sec", "bond", None, None, None))
    return jax.shard_map(shards, mesh=mesh, in_specs=in_specs, out_specs=out_specs, check_vma=False)
```

```python
import jax
import jax.numpy as jnp
from jax import lax
from jax.experimental import pallas as pl
from jax.experimental.pallas import tpu as pltpu
from jax.sharding import PartitionSpec as P

BF = jnp.bfloat16
F32 = jnp.float32
VM = pl.BlockSpec(memory_space=pltpu.VMEM)


LINE = 4
SIZE = LINE * LINE


def turned(b):
    return b % LINE * LINE + b // LINE


def routed(sections, step, ahead=0):
    pairs = []
    for s in range(sections):
        t = (s + ahead) % sections
        for b in range(SIZE):
            pairs.append((SIZE * s + b, SIZE * t + (turned(step(turned(b))) if t % 2 else step(b))))
    return pairs


def along_line(distance):
    return lambda b: b - b % LINE + (b + distance) % LINE


def along_column(distance):
    return lambda b: (b + LINE * distance) % SIZE


def spread_out(local):
    row = lax.broadcasted_iota(jnp.int32, (256, 32), 0)
    col = lax.broadcasted_iota(jnp.int32, (256, 32), 1)
    spread = ((row >> 5) * 4 + (row & 3) == col).astype(BF)
    row = lax.broadcasted_iota(jnp.int32, (32, 256), 0)
    col = lax.broadcasted_iota(jnp.int32, (32, 256), 1)
    copies = (row == (col & 31)).astype(BF)
    kron = jnp.dot(spread, local[...], preferred_element_type=F32).astype(BF)
    kron = jnp.dot(kron, copies, preferred_element_type=F32)
    row = lax.broadcasted_iota(jnp.int32, (256, 256), 0)
    col = lax.broadcasted_iota(jnp.int32, (256, 256), 1)
    kron = jnp.where(((row >> 2) & 7) == (col >> 5), kron, 0.0).astype(BF)
    return kron


def front(own, near, back_, far, cols, local, out, first, second, held, heldc, sems):
    fetches = [pltpu.make_async_copy(ref, held.at[i], sems.at[i]) for i, ref in enumerate((own, near, back_, far))]
    fetches = [pltpu.make_async_copy(cols, heldc, sems.at[4])] + fetches
    for fetch in fetches:
        fetch.start()
    kron = spread_out(local)
    fetches[0].wait()
    cols = heldc
    ket = jnp.concatenate([cols[:, s].reshape(512, 128) for s in range(4)], axis=1)
    for g in range(4):
        fetches[1 + g].wait()
        block = held[g]
        f = jnp.dot(block[:256, :], ket, preferred_element_type=F32)
        for h in range(2):
            part = [f[:, 128 * s : 128 * s + 128].reshape(32, 8, 128) for s in (2 * h, 2 * h + 1)]
            first[32 * g : 32 * g + 32, 16 * h : 16 * h + 16, :] = jnp.concatenate(part, axis=1).astype(BF)
    for blk in range(0, 16, 2):
        f = [first[8 * i : 8 * i + 8].reshape(256, 128) for i in (blk, blk + 1)]
        o = jnp.dot(kron, jnp.concatenate(f, axis=1), preferred_element_type=F32).astype(BF)
        for i in range(2):
            second[:, 32 * (blk + i) : 32 * (blk + i) + 32, :] = o[:, 128 * i : 128 * i + 128].reshape(8, 32, 128)
    site = held[:, 256:, :].reshape(512, 512)
    for n in range(0, 8, 2):
        f = jnp.concatenate([second[n], second[n + 1]], axis=1)
        o = lax.dot_general(site, f, (((0,), (0,)), ((), ())), preferred_element_type=F32).astype(BF)
        for i in range(2):
            out[:, n + i] = o[:, 128 * i : 128 * i + 128].reshape(16, 32, 128)


def back(offsets, left, own, up, down, far_a, far_b, mix, right, out, mixed, proj):
    ket = [left[:, pl.ds(pl.multiple_of(offsets[i], 128), 128)] for i in range(4)]
    ket = jnp.concatenate(ket, axis=1)
    for h in range(8):
        at = slice(512 * h, 512 * h + 512)
        pair = jnp.concatenate([ref[:, at] for ref in (own, up, down, far_a, far_b)], axis=0)
        m = jnp.dot(ket, pair, preferred_element_type=F32)
        part = [m[:, 256 * i : 256 * i + 256].reshape(32, 8, 256) for i in range(2)]
        mixed[:, 16 * h : 16 * h + 16, :] = jnp.concatenate(part, axis=1).astype(BF)
    for p in range(32):
        o = jnp.dot(mix[...], mixed[p], preferred_element_type=F32).astype(BF)
        for k in range(8):
            proj[16 * p : 16 * p + 16, 256 * k : 256 * k + 256] = o[16 * k : 16 * k + 16, :]
    out[...] = jnp.dot(proj[...], right[...], preferred_element_type=F32).astype(BF)


def applied(offsets, left, pieces, mix, right):
    return pl.pallas_call(
        back,
        out_shape=jax.ShapeDtypeStruct((512, 512), BF),
        in_specs=[pl.BlockSpec(memory_space=pltpu.SMEM)] + [VM] * 8,
        out_specs=VM,
        scratch_shapes=[pltpu.VMEM((32, 128, 256), BF), pltpu.VMEM((512, 2048), BF)],
        compiler_params=pltpu.CompilerParams(vmem_limit_bytes=24 << 20),
        cost_estimate=pl.CostEstimate(flops=2_500_000_000, bytes_accessed=8_000_000, transcendentals=0),
        name="back",
    )(offsets, left, *pieces, mix, right)


def shards(left_env, site, psi, right_env, mpo):
    chi = site.shape[-1]
    sections = lax.axis_size("sec")
    here = lax.axis_index("bond")
    odd = lax.axis_index("sec") % 2 == 1
    row = jnp.where(odd, here % LINE, here // LINE)
    column = jnp.where(odd, here // LINE, here % LINE)

    def moved(block, step, ahead=0):
        return lax.ppermute(block, ("sec", "bond"), routed(sections, step, ahead))

    lines = []
    for s in range(sections):
        for y in range(LINE):
            line = [LINE * y + x for x in range(LINE)]
            lines.append([SIZE * s + (turned(b) if s % 2 else b) for b in line])
    own = jnp.concatenate([left_env[0].reshape(256, chi), site[0].reshape(128, chi)], axis=0)
    blocks = [own] + [moved(own, along_line(d)) for d in (1, -1, 2)]
    pair = moved(psi[0], lambda b: b, 1)
    pair, blocks[1], blocks[2] = lax.optimization_barrier((pair, blocks[1], blocks[2]))
    halves = pair.reshape(32, 16, 2, 256).transpose(2, 0, 1, 3).reshape(2, 32, 4096)
    send = jnp.broadcast_to(halves[None], (2, 2, 32, 4096)).reshape(4, 32, 4096)
    pair = lax.all_to_all(send, ("sec", "bond"), 0, 0, axis_index_groups=lines, tiled=True).reshape(128, 4096)
    local = mpo.transpose(1, 3, 2, 0).reshape(32, 32)
    two_site = jnp.einsum("mnsu,nkvw->kuwsvm", mpo, mpo, preferred_element_type=F32)
    two_site = two_site.astype(BF).reshape(128, 128)
    turn = site[0].reshape(32, 4, 4, 4, 32).transpose(0, 1, 3, 2, 4).reshape(32, 4, chi)
    tensor = jnp.where(odd, site[0], turn)
    quarters = tensor.reshape(32, 4, 4, 128).transpose(2, 1, 0, 3)
    cols = jnp.where(odd, quarters[:, None], quarters[None]).reshape(16, 4, 32, 128)
    offsets = (row + jnp.array([0, 3, 1, 2], jnp.int32)) % LINE * 128
    right = lax.dynamic_slice_in_dim(right_env[0], column % 2 * 256, 256, 1).reshape(2048, chi)
    pair, local, two_site, cols, offsets, right = lax.optimization_barrier(
        (pair, local, two_site, cols, offsets, right)
    )
    up = moved(pair, along_column(1))
    down = moved(pair, along_column(-1))
    far_a = moved(up[:64], along_column(1))
    far_b = moved(down[64:], along_column(-1))
    pieces = (pair, up, down, far_a, far_b)
    cols = lax.all_to_all(cols, "bond", 0, 0, tiled=True)
    fresh = pl.pallas_call(
        front,
        out_shape=jax.ShapeDtypeStruct((16, 8, 32, 128), BF),
        in_specs=[pl.BlockSpec(memory_space=pl.ANY)] * 5 + [VM],
        out_specs=VM,
        scratch_shapes=[
            pltpu.VMEM((128, 32, 128), BF),
            pltpu.VMEM((8, 512, 128), BF),
            pltpu.VMEM((4, 384, 512), BF),
            pltpu.VMEM((16, 4, 32, 128), BF),
            pltpu.SemaphoreType.DMA((5,)),
        ],
        compiler_params=pltpu.CompilerParams(vmem_limit_bytes=56 << 20),
        cost_estimate=pl.CostEstimate(flops=2_000_000_000, bytes_accessed=4_000_000, transcendentals=0),
        name="front",
    )(*blocks, cols, local)
    fresh = lax.all_to_all(fresh, "bond", 0, 0, tiled=True).reshape(4, 4, 8, 32, 128)
    fresh = jnp.where(odd, fresh.transpose(1, 0, 2, 3, 4), fresh)
    fresh = [fresh[i].astype(F32) for i in range(4)]
    fresh = ((fresh[0] + fresh[1]) + (fresh[2] + fresh[3])).astype(BF)
    source = fresh.transpose(2, 1, 0, 3).reshape(256, chi)
    i = lax.broadcasted_iota(jnp.int32, (chi, chi), 0)
    j = lax.broadcasted_iota(jnp.int32, (chi, chi), 1)
    place = jnp.where(odd, i, i // 32 % 4 * 128 + i // 128 * 32 + i % 32)
    place = (place == j).astype(BF)
    source, place = lax.optimization_barrier((source, place))
    new_left = jnp.dot(source, place, preferred_element_type=F32).astype(BF).reshape(32, 8, chi)
    other = moved(source, lambda b: b ^ 1, 1)
    source = moved(source, lambda b: b, 1)
    give = applied(offsets, other, pieces, two_site, right)
    source, give = lax.optimization_barrier((source, give))
    take = moved(give, lambda b: b ^ 1)
    keep = applied(offsets, source, pieces, two_site, right)
    total = (keep.astype(F32) + take.astype(F32)).astype(BF)
    return (new_left[None], total.reshape(1, 32, 4, 4, chi))


def solution(mesh):
    in_specs = (
        P("sec", "bond", None, None),
        P("sec", "bond", None, None),
        P("sec", "bond", None, None, None),
        P("sec", None, None, None),
        P(),
    )
    out_specs = (P("sec", "bond", None, None), P("sec", "bond", None, None, None))
    return jax.shard_map(shards, mesh=mesh, in_specs=in_specs, out_specs=out_specs, check_vma=False)
```

```python
import jax
import jax.numpy as jnp
from jax import lax
from jax.experimental import pallas as pl
from jax.experimental.pallas import tpu as pltpu
from jax.sharding import PartitionSpec as P

BF = jnp.bfloat16
F32 = jnp.float32
VM = pl.BlockSpec(memory_space=pltpu.VMEM)


LINE = 4
SIZE = LINE * LINE


def turned(b):
    return b % LINE * LINE + b // LINE


def routed(sections, step, ahead=0):
    pairs = []
    for s in range(sections):
        t = (s + ahead) % sections
        for b in range(SIZE):
            pairs.append((SIZE * s + b, SIZE * t + (turned(step(turned(b))) if t % 2 else step(b))))
    return pairs


def along_line(distance):
    return lambda b: b - b % LINE + (b + distance) % LINE


def along_column(distance):
    return lambda b: (b + LINE * distance) % SIZE


def spread_out(local):
    row = lax.broadcasted_iota(jnp.int32, (256, 32), 0)
    col = lax.broadcasted_iota(jnp.int32, (256, 32), 1)
    spread = ((row >> 5) * 4 + (row & 3) == col).astype(BF)
    row = lax.broadcasted_iota(jnp.int32, (32, 256), 0)
    col = lax.broadcasted_iota(jnp.int32, (32, 256), 1)
    copies = (row == (col & 31)).astype(BF)
    kron = jnp.dot(spread, local[...], preferred_element_type=F32).astype(BF)
    kron = jnp.dot(kron, copies, preferred_element_type=F32)
    row = lax.broadcasted_iota(jnp.int32, (256, 256), 0)
    col = lax.broadcasted_iota(jnp.int32, (256, 256), 1)
    kron = jnp.where(((row >> 2) & 7) == (col >> 5), kron, 0.0).astype(BF)
    return kron


def front(own, near, back_, far, cols, local, out, first, second, held, heldc, sems):
    fetches = [pltpu.make_async_copy(ref, held.at[i], sems.at[i]) for i, ref in enumerate((own, near, back_, far))]
    fetches = [pltpu.make_async_copy(cols, heldc, sems.at[4])] + fetches
    for fetch in fetches:
        fetch.start()
    kron = spread_out(local)
    fetches[0].wait()
    cols = heldc
    ket = jnp.concatenate([cols[:, s].reshape(512, 128) for s in range(4)], axis=1)
    for g in range(4):
        fetches[1 + g].wait()
        block = held[g]
        f = jnp.dot(block[:256, :], ket, preferred_element_type=F32)
        for h in range(2):
            part = [f[:, 128 * s : 128 * s + 128].reshape(32, 8, 128) for s in (2 * h, 2 * h + 1)]
            first[32 * g : 32 * g + 32, 16 * h : 16 * h + 16, :] = jnp.concatenate(part, axis=1).astype(BF)
    for blk in range(0, 16, 2):
        f = [first[8 * i : 8 * i + 8].reshape(256, 128) for i in (blk, blk + 1)]
        o = jnp.dot(kron, jnp.concatenate(f, axis=1), preferred_element_type=F32).astype(BF)
        for i in range(2):
            second[:, 32 * (blk + i) : 32 * (blk + i) + 32, :] = o[:, 128 * i : 128 * i + 128].reshape(8, 32, 128)
    site = held[:, 256:, :].reshape(512, 512)
    for n in range(0, 8, 2):
        f = jnp.concatenate([second[n], second[n + 1]], axis=1)
        o = lax.dot_general(site, f, (((0,), (0,)), ((), ())), preferred_element_type=F32).astype(BF)
        for i in range(2):
            out[:, n + i] = o[:, 128 * i : 128 * i + 128].reshape(16, 32, 128)


def back(offsets, left, own, up, down, far_a, far_b, mix, right, out, mixed, proj):
    ket = [left[:, pl.ds(pl.multiple_of(offsets[i], 128), 128)] for i in range(4)]
    ket = jnp.concatenate(ket, axis=1)
    for h in range(8):
        at = slice(512 * h, 512 * h + 512)
        pair = jnp.concatenate([ref[:, at] for ref in (own, up, down, far_a, far_b)], axis=0)
        m = jnp.dot(ket, pair, preferred_element_type=F32)
        part = [m[:, 256 * i : 256 * i + 256].reshape(32, 8, 256) for i in range(2)]
        mixed[:, 16 * h : 16 * h + 16, :] = jnp.concatenate(part, axis=1).astype(BF)
    for p in range(32):
        o = jnp.dot(mix[...], mixed[p], preferred_element_type=F32).astype(BF)
        for k in range(8):
            proj[16 * p : 16 * p + 16, 256 * k : 256 * k + 256] = o[16 * k : 16 * k + 16, :]
    out[...] = jnp.dot(proj[...], right[...], preferred_element_type=F32).astype(BF)


def applied(offsets, left, pieces, mix, right):
    return pl.pallas_call(
        back,
        out_shape=jax.ShapeDtypeStruct((512, 512), BF),
        in_specs=[pl.BlockSpec(memory_space=pltpu.SMEM)] + [VM] * 8,
        out_specs=VM,
        scratch_shapes=[pltpu.VMEM((32, 128, 256), BF), pltpu.VMEM((512, 2048), BF)],
        compiler_params=pltpu.CompilerParams(vmem_limit_bytes=24 << 20),
        cost_estimate=pl.CostEstimate(flops=2_500_000_000, bytes_accessed=8_000_000, transcendentals=0),
        name="back",
    )(offsets, left, *pieces, mix, right)


def shards(left_env, site, psi, right_env, mpo):
    chi = site.shape[-1]
    sections = lax.axis_size("sec")
    here = lax.axis_index("bond")
    odd = lax.axis_index("sec") % 2 == 1
    row = jnp.where(odd, here % LINE, here // LINE)
    column = jnp.where(odd, here // LINE, here % LINE)

    def moved(block, step, ahead=0):
        return lax.ppermute(block, ("sec", "bond"), routed(sections, step, ahead))

    lines = []
    for s in range(sections):
        for y in range(LINE):
            line = [LINE * y + x for x in range(LINE)]
            lines.append([SIZE * s + (turned(b) if s % 2 else b) for b in line])
    own = jnp.concatenate([left_env[0].reshape(256, chi), site[0].reshape(128, chi)], axis=0)
    blocks = [own] + [moved(own, along_line(d)) for d in (1, -1, 2)]
    pair = moved(psi[0], lambda b: b, 1)
    pair, blocks[1], blocks[2] = lax.optimization_barrier((pair, blocks[1], blocks[2]))
    halves = pair.reshape(32, 16, 2, 256).transpose(2, 0, 1, 3).reshape(2, 32, 4096)
    send = jnp.broadcast_to(halves[None], (2, 2, 32, 4096)).reshape(4, 32, 4096)
    pair = lax.all_to_all(send, ("sec", "bond"), 0, 0, axis_index_groups=lines, tiled=True).reshape(128, 4096)
    local = mpo.transpose(1, 3, 2, 0).reshape(32, 32)
    two_site = jnp.einsum("mnsu,nkvw->kuwsvm", mpo, mpo, preferred_element_type=F32)
    two_site = two_site.astype(BF).reshape(128, 128)
    turn = site[0].reshape(32, 4, 4, 4, 32).transpose(0, 1, 3, 2, 4).reshape(32, 4, chi)
    tensor = jnp.where(odd, site[0], turn)
    quarters = tensor.reshape(32, 4, 4, 128).transpose(2, 1, 0, 3)
    cols = jnp.where(odd, quarters[:, None], quarters[None]).reshape(16, 4, 32, 128)
    offsets = (row + jnp.array([0, 3, 1, 2], jnp.int32)) % LINE * 128
    right = lax.dynamic_slice_in_dim(right_env[0], column % 2 * 256, 256, 1).reshape(2048, chi)
    pair, blocks[3], local, two_site, cols, offsets, right = lax.optimization_barrier(
        (pair, blocks[3], local, two_site, cols, offsets, right)
    )
    up = moved(pair, along_column(1))
    down = moved(pair, along_column(-1))
    far_a = moved(up[:64], along_column(1))
    far_b = moved(down[64:], along_column(-1))
    pieces = (pair, up, down, far_a, far_b)
    cols = lax.all_to_all(cols, "bond", 0, 0, tiled=True)
    fresh = pl.pallas_call(
        front,
        out_shape=jax.ShapeDtypeStruct((16, 8, 32, 128), BF),
        in_specs=[pl.BlockSpec(memory_space=pl.ANY)] * 5 + [VM],
        out_specs=VM,
        scratch_shapes=[
            pltpu.VMEM((128, 32, 128), BF),
            pltpu.VMEM((8, 512, 128), BF),
            pltpu.VMEM((4, 384, 512), BF),
            pltpu.VMEM((16, 4, 32, 128), BF),
            pltpu.SemaphoreType.DMA((5,)),
        ],
        compiler_params=pltpu.CompilerParams(vmem_limit_bytes=56 << 20),
        cost_estimate=pl.CostEstimate(flops=2_000_000_000, bytes_accessed=4_000_000, transcendentals=0),
        name="front",
    )(*blocks, cols, local)
    fresh = lax.all_to_all(fresh, "bond", 0, 0, tiled=True).reshape(4, 4, 8, 32, 128)
    fresh = jnp.where(odd, fresh.transpose(1, 0, 2, 3, 4), fresh)
    fresh = [fresh[i].astype(F32) for i in range(4)]
    fresh = ((fresh[0] + fresh[1]) + (fresh[2] + fresh[3])).astype(BF)
    source = fresh.transpose(2, 1, 0, 3).reshape(256, chi)
    i = lax.broadcasted_iota(jnp.int32, (chi, chi), 0)
    j = lax.broadcasted_iota(jnp.int32, (chi, chi), 1)
    place = jnp.where(odd, i, i // 32 % 4 * 128 + i // 128 * 32 + i % 32)
    place = (place == j).astype(BF)
    source, place = lax.optimization_barrier((source, place))
    new_left = jnp.dot(source, place, preferred_element_type=F32).astype(BF).reshape(32, 8, chi)
    other = moved(source, lambda b: b ^ 1, 1)
    source = moved(source, lambda b: b, 1)
    give = applied(offsets, other, pieces, two_site, right)
    source, give = lax.optimization_barrier((source, give))
    take = moved(give, lambda b: b ^ 1)
    keep = applied(offsets, source, pieces, two_site, right)
    total = (keep.astype(F32) + take.astype(F32)).astype(BF)
    return (new_left[None], total.reshape(1, 32, 4, 4, chi))


def solution(mesh):
    in_specs = (
        P("sec", "bond", None, None),
        P("sec", "bond", None, None),
        P("sec", "bond", None, None, None),
        P("sec", None, None, None),
        P(),
    )
    out_specs = (P("sec", "bond", None, None), P("sec", "bond", None, None, None))
    return jax.shard_map(shards, mesh=mesh, in_specs=in_specs, out_specs=out_specs, check_vma=False)
```

```python
import jax
import jax.numpy as jnp
from jax import lax
from jax.experimental import pallas as pl
from jax.experimental.pallas import tpu as pltpu
from jax.sharding import PartitionSpec as P

BF = jnp.bfloat16
F32 = jnp.float32
VM = pl.BlockSpec(memory_space=pltpu.VMEM)


LINE = 4
SIZE = LINE * LINE


def turned(b):
    return b % LINE * LINE + b // LINE


def routed(sections, step, ahead=0):
    pairs = []
    for s in range(sections):
        t = (s + ahead) % sections
        for b in range(SIZE):
            pairs.append((SIZE * s + b, SIZE * t + (turned(step(turned(b))) if t % 2 else step(b))))
    return pairs


def along_line(distance):
    return lambda b: b - b % LINE + (b + distance) % LINE


def along_column(distance):
    return lambda b: (b + LINE * distance) % SIZE


def spread_out(local):
    row = lax.broadcasted_iota(jnp.int32, (256, 32), 0)
    col = lax.broadcasted_iota(jnp.int32, (256, 32), 1)
    spread = ((row >> 5) * 4 + (row & 3) == col).astype(BF)
    row = lax.broadcasted_iota(jnp.int32, (32, 256), 0)
    col = lax.broadcasted_iota(jnp.int32, (32, 256), 1)
    copies = (row == (col & 31)).astype(BF)
    kron = jnp.dot(spread, local[...], preferred_element_type=F32).astype(BF)
    kron = jnp.dot(kron, copies, preferred_element_type=F32)
    row = lax.broadcasted_iota(jnp.int32, (256, 256), 0)
    col = lax.broadcasted_iota(jnp.int32, (256, 256), 1)
    kron = jnp.where(((row >> 2) & 7) == (col >> 5), kron, 0.0).astype(BF)
    return kron


def front(own, near, back_, far, cols, local, out, first, second, held, heldc, sems):
    fetches = [pltpu.make_async_copy(ref, held.at[i], sems.at[i]) for i, ref in enumerate((own, near, back_, far))]
    fetches = [pltpu.make_async_copy(cols, heldc, sems.at[4])] + fetches
    for fetch in fetches:
        fetch.start()
    kron = spread_out(local)
    fetches[0].wait()
    cols = heldc
    ket = jnp.concatenate([cols[:, s].reshape(512, 128) for s in range(4)], axis=1)
    for g in range(4):
        fetches[1 + g].wait()
        block = held[g]
        f = jnp.dot(block[:256, :], ket, preferred_element_type=F32)
        for h in range(2):
            part = [f[:, 128 * s : 128 * s + 128].reshape(32, 8, 128) for s in (2 * h, 2 * h + 1)]
            first[32 * g : 32 * g + 32, 16 * h : 16 * h + 16, :] = jnp.concatenate(part, axis=1).astype(BF)
    for blk in range(0, 16, 2):
        f = [first[8 * i : 8 * i + 8].reshape(256, 128) for i in (blk, blk + 1)]
        o = jnp.dot(kron, jnp.concatenate(f, axis=1), preferred_element_type=F32).astype(BF)
        for i in range(2):
            second[:, 32 * (blk + i) : 32 * (blk + i) + 32, :] = o[:, 128 * i : 128 * i + 128].reshape(8, 32, 128)
    site = held[:, 256:, :].reshape(512, 512)
    for n in range(0, 8, 2):
        f = jnp.concatenate([second[n], second[n + 1]], axis=1)
        o = lax.dot_general(site, f, (((0,), (0,)), ((), ())), preferred_element_type=F32).astype(BF)
        for i in range(2):
            out[:, n + i] = o[:, 128 * i : 128 * i + 128].reshape(16, 32, 128)


def back(offsets, left, own, up, down, far_a, far_b, mix, right, out, mixed, proj):
    ket = [left[:, pl.ds(pl.multiple_of(offsets[i], 128), 128)] for i in range(4)]
    ket = jnp.concatenate(ket, axis=1)
    for h in range(8):
        at = slice(512 * h, 512 * h + 512)
        pair = jnp.concatenate([ref[:, at] for ref in (own, up, down, far_a, far_b)], axis=0)
        m = jnp.dot(ket, pair, preferred_element_type=F32)
        part = [m[:, 256 * i : 256 * i + 256].reshape(32, 8, 256) for i in range(2)]
        mixed[:, 16 * h : 16 * h + 16, :] = jnp.concatenate(part, axis=1).astype(BF)
    for p in range(32):
        o = jnp.dot(mix[...], mixed[p], preferred_element_type=F32).astype(BF)
        for k in range(8):
            proj[16 * p : 16 * p + 16, 256 * k : 256 * k + 256] = o[16 * k : 16 * k + 16, :]
    out[...] = jnp.dot(proj[...], right[...], preferred_element_type=F32).astype(BF)


def applied(offsets, left, pieces, mix, right):
    return pl.pallas_call(
        back,
        out_shape=jax.ShapeDtypeStruct((512, 512), BF),
        in_specs=[pl.BlockSpec(memory_space=pltpu.SMEM)] + [VM] * 8,
        out_specs=VM,
        scratch_shapes=[pltpu.VMEM((32, 128, 256), BF), pltpu.VMEM((512, 2048), BF)],
        compiler_params=pltpu.CompilerParams(vmem_limit_bytes=24 << 20),
        cost_estimate=pl.CostEstimate(flops=2_500_000_000, bytes_accessed=8_000_000, transcendentals=0),
        name="back",
    )(offsets, left, *pieces, mix, right)


def shards(left_env, site, psi, right_env, mpo):
    chi = site.shape[-1]
    sections = lax.axis_size("sec")
    here = lax.axis_index("bond")
    odd = lax.axis_index("sec") % 2 == 1
    row = jnp.where(odd, here % LINE, here // LINE)
    column = jnp.where(odd, here // LINE, here % LINE)

    def moved(block, step, ahead=0):
        return lax.ppermute(block, ("sec", "bond"), routed(sections, step, ahead))

    lines = []
    for s in range(sections):
        for y in range(LINE):
            line = [LINE * y + x for x in range(LINE)]
            lines.append([SIZE * s + (turned(b) if s % 2 else b) for b in line])
    own = jnp.concatenate([left_env[0].reshape(256, chi), site[0].reshape(128, chi)], axis=0)
    blocks = [own] + [moved(own, along_line(d)) for d in (1, -1, 2)]
    pair = moved(psi[0], lambda b: b, 1)
    pair, blocks[1], blocks[2] = lax.optimization_barrier((pair, blocks[1], blocks[2]))
    halves = pair.reshape(32, 16, 2, 256).transpose(2, 0, 1, 3).reshape(2, 32, 4096)
    send = jnp.broadcast_to(halves[None], (2, 2, 32, 4096)).reshape(4, 32, 4096)
    pair = lax.all_to_all(send, ("sec", "bond"), 0, 0, axis_index_groups=lines, tiled=True).reshape(128, 4096)
    local = mpo.transpose(1, 3, 2, 0).reshape(32, 32)
    two_site = jnp.einsum("mnsu,nkvw->kuwsvm", mpo, mpo, preferred_element_type=F32)
    two_site = two_site.astype(BF).reshape(128, 128)
    turn = site[0].reshape(32, 4, 4, 4, 32).transpose(0, 1, 3, 2, 4).reshape(32, 4, chi)
    tensor = jnp.where(odd, site[0], turn)
    quarters = tensor.reshape(32, 4, 4, 128).transpose(2, 1, 0, 3)
    cols = jnp.where(odd, quarters[:, None], quarters[None]).reshape(16, 4, 32, 128)
    offsets = (row + jnp.array([0, 3, 1, 2], jnp.int32)) % LINE * 128
    right = lax.dynamic_slice_in_dim(right_env[0], column % 2 * 256, 256, 1).reshape(2048, chi)
    i = lax.broadcasted_iota(jnp.int32, (chi, chi), 0)
    j = lax.broadcasted_iota(jnp.int32, (chi, chi), 1)
    place = jnp.where(odd, i, i // 32 % 4 * 128 + i // 128 * 32 + i % 32)
    place = (place == j).astype(BF)
    pair, blocks[3], local, two_site, cols, offsets, right, place = lax.optimization_barrier(
        (pair, blocks[3], local, two_site, cols, offsets, right, place)
    )
    up = moved(pair, along_column(1))
    down = moved(pair, along_column(-1))
    far_a = moved(up[:64], along_column(1))
    far_b = moved(down[64:], along_column(-1))
    pieces = (pair, up, down, far_a, far_b)
    cols = lax.all_to_all(cols, "bond", 0, 0, tiled=True)
    fresh = pl.pallas_call(
        front,
        out_shape=jax.ShapeDtypeStruct((16, 8, 32, 128), BF),
        in_specs=[pl.BlockSpec(memory_space=pl.ANY)] * 5 + [VM],
        out_specs=VM,
        scratch_shapes=[
            pltpu.VMEM((128, 32, 128), BF),
            pltpu.VMEM((8, 512, 128), BF),
            pltpu.VMEM((4, 384, 512), BF),
            pltpu.VMEM((16, 4, 32, 128), BF),
            pltpu.SemaphoreType.DMA((5,)),
        ],
        compiler_params=pltpu.CompilerParams(vmem_limit_bytes=56 << 20),
        cost_estimate=pl.CostEstimate(flops=2_000_000_000, bytes_accessed=4_000_000, transcendentals=0),
        name="front",
    )(*blocks, cols, local)
    fresh = lax.all_to_all(fresh, "bond", 0, 0, tiled=True).reshape(4, 4, 8, 32, 128)
    fresh = jnp.where(odd, fresh.transpose(1, 0, 2, 3, 4), fresh)
    fresh = [fresh[i].astype(F32) for i in range(4)]
    fresh = ((fresh[0] + fresh[1]) + (fresh[2] + fresh[3])).astype(BF)
    source = fresh.transpose(2, 1, 0, 3).reshape(256, chi)
    new_left = jnp.dot(source, place, preferred_element_type=F32).astype(BF).reshape(32, 8, chi)
    other = moved(source, lambda b: b ^ 1, 1)
    source = moved(source, lambda b: b, 1)
    give = applied(offsets, other, pieces, two_site, right)
    source, give = lax.optimization_barrier((source, give))
    take = moved(give, lambda b: b ^ 1)
    keep = applied(offsets, source, pieces, two_site, right)
    total = (keep.astype(F32) + take.astype(F32)).astype(BF)
    return (new_left[None], total.reshape(1, 32, 4, 4, chi))


def solution(mesh):
    in_specs = (
        P("sec", "bond", None, None),
        P("sec", "bond", None, None),
        P("sec", "bond", None, None, None),
        P("sec", None, None, None),
        P(),
    )
    out_specs = (P("sec", "bond", None, None), P("sec", "bond", None, None, None))
    return jax.shard_map(shards, mesh=mesh, in_specs=in_specs, out_specs=out_specs, check_vma=False)
```
